256 devices in a mesh: row: 8 (over z), col: 32 (over y, x, core).
Axes of the slice: x: 4, y: 4, z: 8, core: 2. Of those that a mesh axis runs over, the one named last changes fastest.
Arguments:
- amplitudes: float32 [1024, 131072], P('col', 'row'), may hold values from -6 to 6
- integrals: float32 [131072, 3072], P(('row', 'col')), may hold values from -0.0625 to 0.0625
Outputs:
- ladder: float32 [1024, 3072], P('col', 'row')
The draws below stay inside these ranges and needn't reach their ends.
All inputs are finite; a program needn't handle non-finite values.
Results may differ from the reference program's by a relative error of at most 0.00011.
Values sent between devices are 32-bit elements; how exact they have to be, the bound alone decides.
No kernel may reach another device: no remote copies, remote signals or barrier semaphores. Data moves between devices by JAX's collectives and lax.ppermute only.
A program may use at most 64 MiB of HBM per device.

```python
import jax
import jax.numpy as jnp
from jax import lax

NAB = 3072
NOP = 1024
CD = 131072


def with_spikes(array, stream_key, source, target, parts, factor):
    owner, partner = [(jnp.arange(array.shape[axis_at]) // (array.shape[axis_at] // parts)).reshape([-1 if axis == axis_at else 1 for axis in range(array.ndim)]) for axis_at in (source, target)]
    chosen = jax.random.permutation(stream_key, parts)[partner]
    strong = (owner == chosen) | (owner == (partner + parts // 2) % parts)
    return jnp.where(strong, factor * array, array)


def block_scale(key, extent, pieces, low, high):
    def one(position, shards_of):
        steps = jax.random.uniform(jax.random.fold_in(jax.random.fold_in(key, 6), position), (shards_of,), jnp.float32, low / len(pieces), high / len(pieces))
        return jnp.repeat(jnp.exp(steps), extent[position] // shards_of).reshape((-1,) + (1,) * (len(extent) - position - 1))

    loudness = one(*pieces[0])
    for cut in pieces[1:]:
        loudness = loudness * one(*cut)
    return loudness


def scatter_about(rng, dims, spread, reach, cuts=(), kind=jnp.bfloat16):
    gain = block_scale(rng, dims, cuts, -0.22, 0.18) if cuts else 1.0
    entries = jax.random.normal(rng, dims, jnp.float32) * spread * gain
    return jnp.minimum(jnp.maximum(entries, -reach), reach).astype(kind)


def bell_draw_with(rng, shape, width, bound, pieces, heavy, held_as=jnp.bfloat16):
    values = width * jax.random.normal(rng, shape, jnp.float32)
    if pieces:
        values = values * block_scale(rng, shape, pieces, -0.22, 0.18)
    return jnp.clip(with_spikes(values, jax.random.fold_in(rng, 3), *heavy), -bound, bound).astype(held_as)


def setup_inputs(seed: int = 0) -> dict:
    streams_of = jax.random.split(jax.random.key(seed), 3)
    return {
        "amplitudes": scatter_about(streams_of[0], (NOP, CD), 1.0, 6.0, ((0, 32), (1, 8)), jnp.float32),
        "integrals": bell_draw_with(streams_of[1], (CD, NAB), CD ** -0.5, 0.0625, ((0, 256),), (0, 1, 256, 6.0), jnp.float32),
    }


def reference(amplitudes, integrals):
    product = jnp.dot(amplitudes, integrals, precision=lax.Precision.HIGHEST, preferred_element_type=jnp.float32)
    return 0.5 * product
```

```python
import functools

import jax
import jax.numpy as jnp
from jax import lax
from jax.experimental import pallas as pl
from jax.experimental.pallas import tpu as pltpu
from jax.sharding import Mesh, PartitionSpec as P

AXES = ("z", "y", "x", "core")
NZ, NY, NX = 8, 4, 4
ROWS, DEPTH, WIDTH = 32, 512, 384
GROUPS = 4
NEAR_FIRST, FAR_FIRST = (2, 1, 3, 0), (2, 3, 1, 0)


def flip(axis, mask):
    pairs = []
    for i in range(NZ * NY * NX * 2):
        at = {"z": i // 32, "y": i // 8 % 4, "x": i // 2 % 4, "core": i % 2}
        at[axis] ^= mask
        pairs.append((i, ((at["z"] * 4 + at["y"]) * 4 + at["x"]) * 2 + at["core"]))
    return pairs


def exchange(value, axis, mask):
    return lax.ppermute(value, AXES, flip(axis, mask))


def group_plan(group):
    order, masks = ((NEAR_FIRST, (1, 3)), (FAR_FIRST, (3, 1)))[group % 2]
    first, second = ("x", "y") if group < 2 else ("y", "x")
    steps = [(axis, mask) for axis in (first, second) for mask in masks]
    if first == "x":
        blocks = [qy * 4 + qx for qx in order for qy in order]
    else:
        blocks = [qy * 4 + qx for qy in order for qx in order]
    return steps, blocks


def split(value):
    high = value.astype(jnp.bfloat16)
    return high, (value - high.astype(jnp.float32)).astype(jnp.bfloat16)


def prepare_kernel(where, a_ref, hi_ref, lo_ref):
    own = pl.multiple_of(where[2] * DEPTH, DEPTH)
    other = pl.multiple_of((1 - where[2]) * DEPTH, DEPTH)
    for q in range(NY * NX):
        source = (where[0] ^ (q // 4)) * 4 + (where[1] ^ (q % 4))
        rows = pl.ds(pl.multiple_of(source * ROWS, ROWS), ROWS)
        to = pl.ds(q * ROWS, ROWS)
        for half, start in enumerate((own, other)):
            high, low = split(a_ref[rows, pl.ds(start, DEPTH)])
            hi_ref[to, pl.ds(half * DEPTH, DEPTH)] = high
            lo_ref[to, pl.ds(half * DEPTH, DEPTH)] = low


def prepare(where, a):
    shape = jax.ShapeDtypeStruct(a.shape, jnp.bfloat16)
    return pl.pallas_call(
        prepare_kernel,
        out_shape=(shape, shape),
        in_specs=[pl.BlockSpec(memory_space=pltpu.SMEM), pl.BlockSpec(memory_space=pltpu.VMEM)],
        out_specs=(pl.BlockSpec(memory_space=pltpu.VMEM),) * 2,
        compiler_params=pltpu.CompilerParams(vmem_limit_bytes=16 << 20),
    )(where, a)


def product_kernel(blocks, idx, hi_ref, lo_ref, own0, own1, oth0, oth1, send_ref, keep_ref, bhi, blo):
    for col, (own, oth) in enumerate(((own0, oth0), (own1, oth1))):
        at = pl.ds(col * WIDTH, WIDTH)
        for half, ref in enumerate((own, oth)):
            high, low = split(ref[...])
            bhi[pl.ds(half * DEPTH, DEPTH), at] = high
            blo[pl.ds(half * DEPTH, DEPTH), at] = low
    dot = functools.partial(jnp.dot, preferred_element_type=jnp.float32)
    total = dot(hi_ref[...], bhi[...]) + dot(lo_ref[...], bhi[...]) + dot(hi_ref[...], blo[...])
    for i, q in enumerate(blocks):
        value = total[q * ROWS : (q + 1) * ROWS]
        if i < 8:
            send_ref[pl.ds(i * ROWS, ROWS), :] = value
        else:
            keep_ref[pl.ds((i - 8) * ROWS, ROWS), :] = value


def product(group, idx, hi, lo, own, oth):
    _, blocks = group_plan(group)
    half = jax.ShapeDtypeStruct((8 * ROWS, 2 * WIDTH), jnp.float32)
    whole = pl.BlockSpec((16 * ROWS, 2 * DEPTH), lambda i, idx: (0, 0))
    col = lambda j: pl.BlockSpec((DEPTH, WIDTH), lambda i, idx: (0, idx[2 * group + j]))
    out = pl.BlockSpec((8 * ROWS, 2 * WIDTH), lambda i, idx: (0, 0))
    return pl.pallas_call(
        functools.partial(product_kernel, blocks),
        out_shape=(half, half),
        grid_spec=pltpu.PrefetchScalarGridSpec(
            num_scalar_prefetch=1,
            grid=(1,),
            in_specs=[whole, whole, col(0), col(1), col(0), col(1)],
            out_specs=(out, out),
            scratch_shapes=[pltpu.VMEM((2 * DEPTH, 2 * WIDTH), jnp.bfloat16)] * 2,
        ),
        compiler_params=pltpu.CompilerParams(vmem_limit_bytes=40 << 20),
        cost_estimate=pl.CostEstimate(
            flops=6 * 16 * ROWS * 2 * DEPTH * 2 * WIDTH, bytes_accessed=6 << 20, transcendentals=0
        ),
    )(idx, hi, lo, own, own, oth, oth)


def body(amplitudes, integrals):
    z, y, x, core = (lax.axis_index(name) for name in AXES)
    oth = exchange(integrals, "core", 1)
    mine = lax.all_to_all(amplitudes, ("y", "x"), split_axis=1, concat_axis=0, tiled=True)
    where = jnp.stack([y, x, core]).astype(jnp.int32)
    idx = jnp.stack([z ^ ((k >> 2) | (k & 2) | (k & 1) << 2) for k in range(NZ)]).astype(jnp.int32)
    hi, lo = prepare(where, mine)
    parts = []
    for group in range(GROUPS):
        steps, _ = group_plan(group)
        send, keep = product(group, idx, hi, lo, integrals, oth)
        for axis, mask in steps:
            total = keep + exchange(send, axis, mask)
            half = total.shape[0] // 2
            send, keep = total[:half], total[half:]
        parts.append(total)
    keep = jnp.concatenate(parts[:2], 1) + exchange(jnp.concatenate(parts[2:], 1), "z", 1)
    keep = keep[:, : 2 * WIDTH] + exchange(keep[:, 2 * WIDTH :], "z", 2)
    keep = keep[:, :WIDTH] + exchange(keep[:, WIDTH:], "z", 4)
    return 0.5 * keep


def solution(mesh):
    chips = Mesh(mesh.devices.reshape(NZ, NY, NX, 2), AXES)
    return jax.shard_map(
        body,
        mesh=chips,
        in_specs=(P(("y", "x", "core"), "z"), P(AXES, None)),
        out_specs=P(("y", "x", "core"), "z"),
        check_vma=False,
    )
```

```python
import functools

import jax
import jax.numpy as jnp
from jax import lax
from jax.experimental import pallas as pl
from jax.experimental.pallas import tpu as pltpu
from jax.sharding import Mesh, PartitionSpec as P

AXES = ("z", "y", "x", "core")
NZ, NY, NX = 8, 4, 4
ROWS, DEPTH, WIDTH = 32, 512, 384
GROUPS = 4
NEAR_FIRST, FAR_FIRST = (2, 1, 3, 0), (2, 3, 1, 0)


def flip(axis, mask):
    pairs = []
    for i in range(NZ * NY * NX * 2):
        at = {"z": i // 32, "y": i // 8 % 4, "x": i // 2 % 4, "core": i % 2}
        at[axis] ^= mask
        pairs.append((i, ((at["z"] * 4 + at["y"]) * 4 + at["x"]) * 2 + at["core"]))
    return pairs


def exchange(value, axis, mask):
    return lax.ppermute(value, AXES, flip(axis, mask))


def group_plan(group):
    order, masks = ((NEAR_FIRST, (1, 3)), (FAR_FIRST, (3, 1)))[group % 2]
    first, second = ("x", "y") if group < 2 else ("y", "x")
    steps = [(axis, mask) for axis in (first, second) for mask in masks]
    if first == "x":
        blocks = [qy * 4 + qx for qx in order for qy in order]
    else:
        blocks = [qy * 4 + qx for qy in order for qx in order]
    return steps, blocks


def split(value):
    high = value.astype(jnp.bfloat16)
    return high, (value - high.astype(jnp.float32)).astype(jnp.bfloat16)


def prepare_kernel(where, a_ref, hi_ref, lo_ref):
    own = pl.multiple_of(where[2] * DEPTH, DEPTH)
    other = pl.multiple_of((1 - where[2]) * DEPTH, DEPTH)
    for q in range(NY * NX):
        source = (where[0] ^ (q // 4)) * 4 + (where[1] ^ (q % 4))
        rows = pl.ds(pl.multiple_of(source * ROWS, ROWS), ROWS)
        to = pl.ds(q * ROWS, ROWS)
        for half, start in enumerate((own, other)):
            high, low = split(a_ref[rows, pl.ds(start, DEPTH)])
            hi_ref[to, pl.ds(half * DEPTH, DEPTH)] = high
            lo_ref[to, pl.ds(half * DEPTH, DEPTH)] = low


def prepare(where, a):
    shape = jax.ShapeDtypeStruct(a.shape, jnp.bfloat16)
    return pl.pallas_call(
        prepare_kernel,
        out_shape=(shape, shape),
        in_specs=[pl.BlockSpec(memory_space=pltpu.SMEM), pl.BlockSpec(memory_space=pltpu.VMEM)],
        out_specs=(pl.BlockSpec(memory_space=pltpu.VMEM),) * 2,
        compiler_params=pltpu.CompilerParams(vmem_limit_bytes=16 << 20),
    )(where, a)


def integrals_kernel(idx, own_ref, oth_ref, hi_ref, lo_ref):
    for half, ref in enumerate((own_ref, oth_ref)):
        to = pl.ds(half * DEPTH, DEPTH)
        hi_ref[to, :], lo_ref[to, :] = split(ref[...])


def prepare_integrals(idx, own, oth):
    shape = jax.ShapeDtypeStruct((2 * DEPTH, NZ * WIDTH), jnp.bfloat16)
    block = pl.BlockSpec((DEPTH, WIDTH), lambda k, idx: (0, idx[k]))
    out = pl.BlockSpec((2 * DEPTH, WIDTH), lambda k, idx: (0, k))
    return pl.pallas_call(
        integrals_kernel,
        out_shape=(shape, shape),
        grid_spec=pltpu.PrefetchScalarGridSpec(
            num_scalar_prefetch=1, grid=(NZ,), in_specs=[block, block], out_specs=(out, out)
        ),
        compiler_params=pltpu.CompilerParams(vmem_limit_bytes=16 << 20),
        cost_estimate=pl.CostEstimate(flops=20 << 20, bytes_accessed=24 << 20, transcendentals=0),
    )(idx, own, oth)


def product_kernel(group, hi_ref, lo_ref, bhi_ref, blo_ref, send_ref, keep_ref):
    _, blocks = group_plan(group)
    cols = pl.ds(group * 2 * WIDTH, 2 * WIDTH)
    dot = functools.partial(jnp.dot, preferred_element_type=jnp.float32)
    total = dot(hi_ref[...], bhi_ref[:, cols])
    total += dot(lo_ref[...], bhi_ref[:, cols])
    total += dot(hi_ref[...], blo_ref[:, cols])
    for i, q in enumerate(blocks):
        value = total[q * ROWS : (q + 1) * ROWS]
        if i < 8:
            send_ref[pl.ds(i * ROWS, ROWS), :] = value
        else:
            keep_ref[pl.ds((i - 8) * ROWS, ROWS), :] = value


def product(group, hi, lo, bhi, blo):
    half = jax.ShapeDtypeStruct((8 * ROWS, 2 * WIDTH), jnp.float32)
    vmem = pl.BlockSpec(memory_space=pltpu.VMEM)
    return pl.pallas_call(
        functools.partial(product_kernel, group),
        out_shape=(half, half),
        in_specs=[vmem] * 4,
        out_specs=(vmem, vmem),
        compiler_params=pltpu.CompilerParams(vmem_limit_bytes=32 << 20),
        cost_estimate=pl.CostEstimate(
            flops=6 * 16 * ROWS * 2 * DEPTH * 2 * WIDTH, bytes_accessed=6 << 20, transcendentals=0
        ),
    )(hi, lo, bhi, blo)


def body(amplitudes, integrals):
    z, y, x, core = (lax.axis_index(name) for name in AXES)
    oth = exchange(integrals, "core", 1)
    mine = lax.all_to_all(amplitudes, ("y", "x"), split_axis=1, concat_axis=0, tiled=True)
    where = jnp.stack([y, x, core]).astype(jnp.int32)
    idx = jnp.stack([z ^ ((k >> 2) | (k & 2) | (k & 1) << 2) for k in range(NZ)]).astype(jnp.int32)
    bhi, blo = prepare_integrals(idx, integrals, oth)
    hi, lo = prepare(where, mine)
    parts = []
    for group in range(GROUPS):
        steps, _ = group_plan(group)
        send, keep = product(group, hi, lo, bhi, blo)
        for axis, mask in steps:
            total = keep + exchange(send, axis, mask)
            half = total.shape[0] // 2
            send, keep = total[:half], total[half:]
        parts.append(total)
    keep = jnp.concatenate(parts[:2], 1) + exchange(jnp.concatenate(parts[2:], 1), "z", 1)
    keep = keep[:, : 2 * WIDTH] + exchange(keep[:, 2 * WIDTH :], "z", 2)
    keep = keep[:, :WIDTH] + exchange(keep[:, WIDTH:], "z", 4)
    return 0.5 * keep


def solution(mesh):
    chips = Mesh(mesh.devices.reshape(NZ, NY, NX, 2), AXES)
    return jax.shard_map(
        body,
        mesh=chips,
        in_specs=(P(("y", "x", "core"), "z"), P(AXES, None)),
        out_specs=P(("y", "x", "core"), "z"),
        check_vma=False,
    )
```

```python
import functools

import jax
import jax.numpy as jnp
from jax import lax
from jax.experimental import pallas as pl
from jax.experimental.pallas import tpu as pltpu
from jax.sharding import Mesh, PartitionSpec as P

AXES = ("z", "y", "x", "core")
NZ, NY, NX = 8, 4, 4
ROWS, DEPTH, WIDTH = 32, 512, 384
GROUPS = 4
NEAR_FIRST, FAR_FIRST = (2, 1, 3, 0), (2, 3, 1, 0)
LAID = (1, 2, 3, 0, 1)
CHEAP = pl.CostEstimate(flops=1 << 20, bytes_accessed=1 << 16, transcendentals=0)
VMEM = pl.BlockSpec(memory_space=pltpu.VMEM)


def flip(axis, mask):
    pairs = []
    for i in range(NZ * NY * NX * 2):
        at = {"z": i // 32, "y": i // 8 % 4, "x": i // 2 % 4, "core": i % 2}
        at[axis] ^= mask
        pairs.append((i, ((at["z"] * 4 + at["y"]) * 4 + at["x"]) * 2 + at["core"]))
    return pairs


def exchange(value, axis, mask):
    return lax.ppermute(value, AXES, flip(axis, mask))


def split(value):
    high = value.astype(jnp.bfloat16)
    return high, (value - high.astype(jnp.float32)).astype(jnp.bfloat16)


def relayout_kernel(a_ref, out_ref):
    for i in range(NY * NX):
        out_ref[i] = a_ref[:, pl.ds(i * 2 * DEPTH, 2 * DEPTH)]


def relayout(a):
    return pl.pallas_call(
        relayout_kernel,
        out_shape=jax.ShapeDtypeStruct((NY * NX, ROWS, 2 * DEPTH), jnp.float32),
        in_specs=[VMEM],
        out_specs=VMEM,
        compiler_params=pltpu.CompilerParams(vmem_limit_bytes=4 << 20),
        cost_estimate=CHEAP,
    )(a)


def prepare_kernel(outer, where, a_ref, b_ref, hi_ref, lo_ref, b0_ref, b1_ref, sems):
    copies = []
    for i, to in enumerate((b0_ref, b1_ref)):
        group = i if outer == "x" else i + 2
        cols = pl.ds(group * 2 * WIDTH, 2 * WIDTH)
        copies.append(pltpu.make_async_copy(b_ref.at[:, cols], to, sems.at[i]))
        copies[i].start()
    own = pl.multiple_of(where[2] * DEPTH, DEPTH)
    other = pl.multiple_of((1 - where[2]) * DEPTH, DEPTH)
    for i in range(5 * 4):
        q = (LAID[i // 4], LAID[i % 4])
        qy, qx = q if outer == "y" else q[::-1]
        source = (where[0] ^ qy) * 4 + (where[1] ^ qx)
        rows = pl.ds(pl.multiple_of(source * ROWS, ROWS), ROWS)
        to = pl.ds(i * ROWS, ROWS)
        for half, start in enumerate((own, other)):
            high, low = split(a_ref[rows, pl.ds(start, DEPTH)])
            hi_ref[to, pl.ds(half * DEPTH, DEPTH)] = high
            lo_ref[to, pl.ds(half * DEPTH, DEPTH)] = low
    for copy in copies:
        copy.wait()


def prepare(outer, where, a, oth):
    part = jax.ShapeDtypeStruct((20 * ROWS, 2 * DEPTH), jnp.bfloat16)
    cols = jax.ShapeDtypeStruct((DEPTH, 2 * WIDTH), jnp.float32)
    hi, lo, *b = pl.pallas_call(
        functools.partial(prepare_kernel, outer),
        out_shape=(part, part, cols, cols),
        in_specs=[pl.BlockSpec(memory_space=pltpu.SMEM), VMEM, pl.BlockSpec(memory_space=pl.ANY)],
        out_specs=(VMEM,) * 4,
        scratch_shapes=[pltpu.SemaphoreType.DMA((2,))],
        compiler_params=pltpu.CompilerParams(vmem_limit_bytes=10 << 20),
        cost_estimate=CHEAP,
    )(where, a, oth)
    return (hi, lo), b


def product_kernel(group, first, order, hi_ref, lo_ref, own_ref, oth_ref, out_ref):
    rows = pl.ds(first * 4 * ROWS, 8 * ROWS)
    cols = pl.ds(group * 2 * WIDTH, 2 * WIDTH)
    dot = functools.partial(jnp.dot, preferred_element_type=jnp.float32)
    total = None
    for half, ref in enumerate((own_ref, oth_ref)):
        depth = pl.ds(half * DEPTH, DEPTH)
        a_hi, a_lo = hi_ref[rows, depth], lo_ref[rows, depth]
        b_hi, b_lo = split(ref[...] if half else ref[:, cols])
        part = dot(a_hi, b_hi) + dot(a_lo, b_hi) + dot(a_hi, b_lo)
        total = part if total is None else total + part
    for i, at in enumerate(order):
        out_ref[pl.ds(i * ROWS, ROWS), :] = total[at * ROWS : (at + 1) * ROWS]


def half_plan(group, half):
    blocks = (NEAR_FIRST, FAR_FIRST)[group % 2]
    outer = blocks[2 * half : 2 * half + 2]
    first = min(f for f in range(4) if set(LAID[f : f + 2]) == set(outer))
    laid = [(o, i) for o in LAID[first : first + 2] for i in LAID[:4]]
    return first, [laid.index((o, i)) for o in outer for i in blocks]


def product(group, half, a, own, oth):
    return pl.pallas_call(
        functools.partial(product_kernel, group, *half_plan(group, half)),
        out_shape=jax.ShapeDtypeStruct((8 * ROWS, 2 * WIDTH), jnp.float32),
        in_specs=[VMEM] * 4,
        out_specs=VMEM,
        compiler_params=pltpu.CompilerParams(vmem_limit_bytes=6 << 20),
        cost_estimate=CHEAP,
    )(*a, own, oth)


def body(amplitudes, integrals):
    z, y, x, core = (lax.axis_index(name) for name in AXES)
    oth = exchange(integrals, "core", 1)
    where = jnp.stack([y, x, core]).astype(jnp.int32)
    halves = [((z & 1) ^ v) * 4 * WIDTH for v in range(2)]
    blocks = [((z >> 1) ^ v) * WIDTH for v in range(4)]
    where, halves, blocks, laid = lax.optimization_barrier((where, halves, blocks, relayout(amplitudes)))
    mine = lax.all_to_all(laid, ("y", "x"), split_axis=0, concat_axis=0)
    mine = mine.reshape(NY * NX * ROWS, 2 * DEPTH)
    a_x, oth_x = prepare("x", where, mine, oth)
    a_y, oth_y = prepare("y", where, mine, oth)
    parts = []
    for group in range(GROUPS):
        a = a_x if group < 2 else a_y
        masks = ((1, 3), (3, 1))[group % 2]
        b = (oth_x + oth_y)[group]
        send = product(group, 0, a, integrals, b)
        keep = product(group, 1, a, integrals, b)
        for axis in ("x", "y") if group < 2 else ("y", "x"):
            for mask in masks:
                total = keep + exchange(send, axis, mask)
                half = total.shape[0] // 2
                send, keep = total[:half], total[half:]
        parts.append(total)
    cut = functools.partial(lax.dynamic_slice_in_dim, axis=1, allow_negative_indices=False)
    parts = [part[:, i * WIDTH : (i + 1) * WIDTH] for i in range(2) for part in parts]
    both = jnp.concatenate(parts, 1)
    keep, send = (cut(both, start, 4 * WIDTH) for start in halves)
    keep = keep + exchange(send, "z", 1)
    block = lambda v: cut(keep, blocks[v], WIDTH)
    far = [exchange(block(v), "z", 2 * v) for v in (2, 1, 3)]
    return 0.5 * (block(0) + far[0] + far[1] + far[2])


def solution(mesh):
    chips = Mesh(mesh.devices.reshape(NZ, NY, NX, 2), AXES)
    return jax.shard_map(
        body,
        mesh=chips,
        in_specs=(P(("y", "x", "core"), "z"), P(AXES, None)),
        out_specs=P(("y", "x", "core"), "z"),
        check_vma=False,
    )
```

```python
import functools

import jax
import jax.numpy as jnp
from jax import lax
from jax.experimental import pallas as pl
from jax.experimental.pallas import tpu as pltpu
from jax.sharding import Mesh, PartitionSpec as P

AXES = ("z", "y", "x", "core")
NZ, NY, NX = 8, 4, 4
ROWS, DEPTH, WIDTH = 32, 512, 384
GROUPS = 4
NEAR_FIRST, FAR_FIRST = (2, 1, 3, 0), (2, 3, 1, 0)
SECOND = (1, 3, 2, 0)
CHEAP = pl.CostEstimate(flops=1 << 20, bytes_accessed=1 << 16, transcendentals=0)
VMEM = pl.BlockSpec(memory_space=pltpu.VMEM)


def flip(axis, mask):
    pairs = []
    for i in range(NZ * NY * NX * 2):
        at = {"z": i // 32, "y": i // 8 % 4, "x": i // 2 % 4, "core": i % 2}
        at[axis] ^= mask
        pairs.append((i, ((at["z"] * 4 + at["y"]) * 4 + at["x"]) * 2 + at["core"]))
    return pairs


def exchange(value, axis, mask):
    return lax.ppermute(value, AXES, flip(axis, mask))


def split(value):
    high = value.astype(jnp.bfloat16)
    return high, (value - high.astype(jnp.float32)).astype(jnp.bfloat16)


def relayout_kernel(a_ref, out_ref):
    for i in range(NY * NX):
        out_ref[i] = a_ref[:, pl.ds(i * 2 * DEPTH, 2 * DEPTH)]


def relayout(a):
    return pl.pallas_call(
        relayout_kernel,
        out_shape=jax.ShapeDtypeStruct((NY * NX, ROWS, 2 * DEPTH), jnp.float32),
        in_specs=[VMEM],
        out_specs=VMEM,
        compiler_params=pltpu.CompilerParams(vmem_limit_bytes=4 << 20),
        cost_estimate=CHEAP,
    )(a)


def after(value, *earlier):
    return lax.optimization_barrier((value, *earlier))[0]


def columns(group):
    return pl.ds(group * 2 * WIDTH, 2 * WIDTH)


def multiply(group, half, other, hi_ref, lo_ref, b):
    blocks = (NEAR_FIRST, FAR_FIRST)[group % 2]
    order = [(outer, inner) for outer in blocks[2 * half : 2 * half + 2] for inner in SECOND]
    order = [qy * 4 + qx if group < 2 else qx * 4 + qy for qx, qy in order]
    depth = pl.ds(other * DEPTH, DEPTH)
    a_hi, a_lo = (
        jnp.concatenate([ref[q * ROWS : (q + 1) * ROWS, depth] for q in order], 0)
        for ref in (hi_ref, lo_ref)
    )
    b_hi, b_lo = split(b)
    dot = functools.partial(jnp.dot, preferred_element_type=jnp.float32)
    return dot(a_hi, b_hi) + dot(a_lo, b_hi) + dot(a_hi, b_lo)


def whole(group, half, hi_ref, lo_ref, own_ref, oth_ref):
    total = multiply(group, half, 0, hi_ref, lo_ref, own_ref[:, columns(group)])
    return total + multiply(group, half, 1, hi_ref, lo_ref, oth_ref[:, columns(group)])


def sent_kernel(where, a_ref, own_ref, oth_ref, *refs):
    *outs, hi_ref, lo_ref = refs
    for q in range(NY * NX):
        source = (where[0] ^ (q // 4)) * 4 + (where[1] ^ (q % 4))
        rows = pl.ds(pl.multiple_of(source * ROWS, ROWS), ROWS)
        to = pl.ds(q * ROWS, ROWS)
        for other in range(2):
            depth = pl.ds(pl.multiple_of((where[2] ^ other) * DEPTH, DEPTH), DEPTH)
            high, low = split(a_ref[rows, depth])
            hi_ref[to, pl.ds(other * DEPTH, DEPTH)] = high
            lo_ref[to, pl.ds(other * DEPTH, DEPTH)] = low
    for group, out_ref in enumerate(outs):
        out_ref[...] = whole(group, 0, hi_ref, lo_ref, own_ref, oth_ref)


def kept_kernel(group, *refs):
    *refs, out_ref = refs
    out_ref[...] = whole(group, 1, *refs)


def call(kernel, out_shape, in_specs, limit):
    return pl.pallas_call(
        kernel,
        out_shape=out_shape,
        in_specs=in_specs,
        out_specs=jax.tree.map(lambda _: VMEM, out_shape),
        compiler_params=pltpu.CompilerParams(vmem_limit_bytes=limit << 20),
        cost_estimate=CHEAP,
    )


def products(where, a, own, oth):
    out = jax.ShapeDtypeStruct((8 * ROWS, 2 * WIDTH), jnp.float32)
    part = jax.ShapeDtypeStruct((NY * NX * ROWS, 2 * DEPTH), jnp.bfloat16)
    smem = pl.BlockSpec(memory_space=pltpu.SMEM)
    *sends, hi, lo = call(
        sent_kernel, (out,) * GROUPS + (part, part), [smem, VMEM, VMEM, VMEM], 6
    )(where, a, own, oth)
    keeps = [
        call(functools.partial(kept_kernel, group), out, [VMEM] * 4, 6)(hi, lo, own, oth)
        for group in range(GROUPS)
    ]
    return sends, keeps


def body(amplitudes, integrals):
    z, y, x, core = (lax.axis_index(name) for name in AXES)
    where = jnp.stack([y, x, core]).astype(jnp.int32)
    halves = [((z & 1) ^ v) * 4 * WIDTH for v in range(2)]
    blocks = [((z >> 1) ^ v) * WIDTH for v in range(4)]
    scalars = (where, halves, blocks)
    scalars, amplitudes, integrals = lax.optimization_barrier((scalars, amplitudes, integrals))
    where, halves, blocks = scalars
    oth = exchange(integrals, "core", 1)
    laid = relayout(amplitudes)
    mine = lax.all_to_all(laid, ("y", "x"), split_axis=0, concat_axis=0)
    mine = mine.reshape(NY * NX * ROWS, 2 * DEPTH)
    sends, parts = products(where, mine, integrals, oth)
    parts[0] = after(parts[0], *parts[1:])
    last = None
    for step in range(2):
        for group in range(GROUPS):
            keep = parts[group] if last is None else after(parts[group], last)
            mask = ((1, 3), (3, 1))[group % 2][step]
            last = keep + exchange(sends[group], "xxyy"[group], mask)
            if step == 0:
                sends[group], parts[group] = last[: 4 * ROWS], last[4 * ROWS :]
            else:
                parts[group] = last
    pairs = []
    for first, axis in ((0, "y"), (2, "x")):
        pair = [
            jnp.concatenate([part[i * ROWS : (i + 1) * ROWS] for part in parts[first : first + 2]], 1)
            for i in range(4)
        ]
        pairs.append(pair[3] + sum(exchange(pair[i], axis, SECOND[i]) for i in range(3)))
    cut = functools.partial(lax.dynamic_slice_in_dim, axis=1, allow_negative_indices=False)
    order = [(pair, i) for parity in range(2) for pair in pairs for i in (parity, parity + 2)]
    both = jnp.concatenate([pair[:, i * WIDTH : (i + 1) * WIDTH] for pair, i in order], 1)
    keep, send = (cut(both, start, 4 * WIDTH) for start in halves)
    keep = keep + exchange(send, "z", 1)
    block = lambda v: cut(keep, blocks[v], WIDTH)
    far = [exchange(block(v), "z", 2 * v) for v in (2, 1, 3)]
    return 0.5 * (block(0) + far[0] + far[1] + far[2])


def solution(mesh):
    chips = Mesh(mesh.devices.reshape(NZ, NY, NX, 2), AXES)
    return jax.shard_map(
        body,
        mesh=chips,
        in_specs=(P(("y", "x", "core"), "z"), P(AXES, None)),
        out_specs=P(("y", "x", "core"), "z"),
        check_vma=False,
    )
```

```python
import functools

import jax
import jax.numpy as jnp
from jax import lax
from jax.experimental import pallas as pl
from jax.experimental.pallas import tpu as pltpu
from jax.sharding import Mesh, PartitionSpec as P

AXES = ("z", "y", "x", "core")
NZ, NY, NX = 8, 4, 4
ROWS, DEPTH, WIDTH = 32, 512, 384
GROUPS = 4
NEAR_FIRST, FAR_FIRST = (2, 1, 3, 0), (2, 3, 1, 0)
SECOND = (1, 3, 2, 0)
CHEAP = pl.CostEstimate(flops=1 << 20, bytes_accessed=1 << 16, transcendentals=0)
VMEM = pl.BlockSpec(memory_space=pltpu.VMEM)


def flip(axis, mask):
    pairs = []
    for i in range(NZ * NY * NX * 2):
        at = {"z": i // 32, "y": i // 8 % 4, "x": i // 2 % 4, "core": i % 2}
        at[axis] ^= mask
        pairs.append((i, ((at["z"] * 4 + at["y"]) * 4 + at["x"]) * 2 + at["core"]))
    return pairs


def exchange(value, axis, mask):
    return lax.ppermute(value, AXES, flip(axis, mask))


def split(value):
    high = value.astype(jnp.bfloat16)
    return high, (value - high.astype(jnp.float32)).astype(jnp.bfloat16)


def relayout_kernel(a_ref, out_ref):
    for i in range(NY * NX):
        out_ref[i] = a_ref[:, pl.ds(i * 2 * DEPTH, 2 * DEPTH)]


def relayout(a):
    return pl.pallas_call(
        relayout_kernel,
        out_shape=jax.ShapeDtypeStruct((NY * NX, ROWS, 2 * DEPTH), jnp.float32),
        in_specs=[VMEM],
        out_specs=VMEM,
        compiler_params=pltpu.CompilerParams(vmem_limit_bytes=4 << 20),
        cost_estimate=CHEAP,
    )(a)


def after(value, *earlier):
    return lax.optimization_barrier((value, *earlier))[0]


def columns(group):
    return pl.ds(group * 2 * WIDTH, 2 * WIDTH)


def multiply(group, half, other, hi_ref, lo_ref, b):
    blocks = (NEAR_FIRST, FAR_FIRST)[group % 2]
    order = [(outer, inner) for outer in blocks[2 * half : 2 * half + 2] for inner in SECOND]
    order = [qy * 4 + qx if group < 2 else qx * 4 + qy for qx, qy in order]
    depth = pl.ds(other * DEPTH, DEPTH)
    a_hi, a_lo = (
        jnp.concatenate([ref[q * ROWS : (q + 1) * ROWS, depth] for q in order], 0)
        for ref in (hi_ref, lo_ref)
    )
    b_hi, b_lo = split(b)
    dot = functools.partial(jnp.dot, preferred_element_type=jnp.float32)
    return dot(a_hi, b_hi) + dot(a_lo, b_hi) + dot(a_hi, b_lo)


def whole(group, half, hi_ref, lo_ref, own_ref, oth_ref):
    total = multiply(group, half, 0, hi_ref, lo_ref, own_ref[:, columns(group)])
    return total + multiply(group, half, 1, hi_ref, lo_ref, oth_ref[:, columns(group)])


def first_kernel(where, a_ref, own_ref, oth_ref, *refs):
    *outs, hi_ref, lo_ref = refs
    for q in range(NY * NX):
        source = (where[0] ^ (q // 4)) * 4 + (where[1] ^ (q % 4))
        rows = pl.ds(pl.multiple_of(source * ROWS, ROWS), ROWS)
        to = pl.ds(q * ROWS, ROWS)
        for other in range(2):
            depth = pl.ds(pl.multiple_of((where[2] ^ other) * DEPTH, DEPTH), DEPTH)
            high, low = split(a_ref[rows, depth])
            hi_ref[to, pl.ds(other * DEPTH, DEPTH)] = high
            lo_ref[to, pl.ds(other * DEPTH, DEPTH)] = low
    for group, out_ref in enumerate(outs):
        out_ref[...] = whole(group, 0, hi_ref, lo_ref, own_ref, oth_ref)


def product_kernel(groups, half, *refs):
    for group, out_ref in zip(groups, refs[4:]):
        out_ref[...] = whole(group, half, *refs[:4])


def call(kernel, out_shape, in_specs, limit):
    return pl.pallas_call(
        kernel,
        out_shape=out_shape,
        in_specs=in_specs,
        out_specs=jax.tree.map(lambda _: VMEM, out_shape),
        compiler_params=pltpu.CompilerParams(vmem_limit_bytes=limit << 20),
        cost_estimate=CHEAP,
    )


def products(where, a, own, oth):
    out = jax.ShapeDtypeStruct((8 * ROWS, 2 * WIDTH), jnp.float32)
    part = jax.ShapeDtypeStruct((NY * NX * ROWS, 2 * DEPTH), jnp.bfloat16)
    smem = pl.BlockSpec(memory_space=pltpu.SMEM)
    *sends, hi, lo = call(
        first_kernel, (out,) * 2 + (part, part), [smem, VMEM, VMEM, VMEM], 6
    )(where, a, own, oth)
    later = functools.partial(product_kernel, (2, 3), 0)
    sends += call(later, (out,) * 2, [VMEM] * 4, 6)(hi, lo, own, oth)
    hi = after(hi, sends[-1])
    keeps = []
    for group in range(GROUPS):
        kernel = functools.partial(product_kernel, (group,), 1)
        keeps += call(kernel, (out,), [VMEM] * 4, 6)(hi, lo, own, oth)
    return sends, keeps


def body(amplitudes, integrals):
    z, y, x, core = (lax.axis_index(name) for name in AXES)
    where = jnp.stack([y, x, core]).astype(jnp.int32)
    halves = [((z & 1) ^ v) * 4 * WIDTH for v in range(2)]
    blocks = [((z >> 1) ^ v) * WIDTH for v in range(4)]
    scalars = (where, halves, blocks)
    scalars, amplitudes, integrals = lax.optimization_barrier((scalars, amplitudes, integrals))
    where, halves, blocks = scalars
    oth = exchange(integrals, "core", 1)
    laid = relayout(amplitudes)
    mine = lax.all_to_all(laid, ("y", "x"), split_axis=0, concat_axis=0)
    mine = mine.reshape(NY * NX * ROWS, 2 * DEPTH)
    sends, parts = products(where, mine, integrals, oth)
    parts[0] = after(parts[0], *parts[1:])
    last = None
    for step in range(2):
        for group in range(GROUPS):
            keep = parts[group] if last is None else after(parts[group], last)
            mask = ((1, 3), (3, 1))[group % 2][step]
            last = keep + exchange(sends[group], "xxyy"[group], mask)
            if step == 0:
                sends[group], parts[group] = last[: 4 * ROWS], last[4 * ROWS :]
            else:
                parts[group] = last
    pairs = []
    for first, axis in ((0, "y"), (2, "x")):
        pair = [
            jnp.concatenate([part[i * ROWS : (i + 1) * ROWS] for part in parts[first : first + 2]], 1)
            for i in range(4)
        ]
        pairs.append(pair[3] + sum(exchange(pair[i], axis, SECOND[i]) for i in range(3)))
    cut = functools.partial(lax.dynamic_slice_in_dim, axis=1, allow_negative_indices=False)
    order = [(pair, i) for parity in range(2) for pair in pairs for i in (parity, parity + 2)]
    both = jnp.concatenate([pair[:, i * WIDTH : (i + 1) * WIDTH] for pair, i in order], 1)
    keep, send = (cut(both, start, 4 * WIDTH) for start in halves)
    keep = keep + exchange(send, "z", 1)
    block = lambda v: cut(keep, blocks[v], WIDTH)
    far = [exchange(block(v), "z", 2 * v) for v in (2, 1, 3)]
    return 0.5 * (block(0) + far[0] + far[1] + far[2])


def solution(mesh):
    chips = Mesh(mesh.devices.reshape(NZ, NY, NX, 2), AXES)
    return jax.shard_map(
        body,
        mesh=chips,
        in_specs=(P(("y", "x", "core"), "z"), P(AXES, None)),
        out_specs=P(("y", "x", "core"), "z"),
        check_vma=False,
    )
```

```python
import functools

import jax
import jax.numpy as jnp
from jax import lax
from jax.experimental import pallas as pl
from jax.experimental.pallas import tpu as pltpu
from jax.sharding import Mesh, PartitionSpec as P

AXES = ("z", "y", "x", "core")
NZ, NY, NX = 8, 4, 4
ROWS, DEPTH, WIDTH = 32, 512, 384
GROUPS = 4
NEAR_FIRST, FAR_FIRST = (2, 1, 3, 0), (2, 3, 1, 0)
SECOND = (2, 1, 3, 0)
CHEAP = pl.CostEstimate(flops=1 << 20, bytes_accessed=1 << 16, transcendentals=0)
VMEM = pl.BlockSpec(memory_space=pltpu.VMEM)


def flip(axis, mask):
    pairs = []
    for i in range(NZ * NY * NX * 2):
        at = {"z": i // 32, "y": i // 8 % 4, "x": i // 2 % 4, "core": i % 2}
        at[axis] ^= mask
        pairs.append((i, ((at["z"] * 4 + at["y"]) * 4 + at["x"]) * 2 + at["core"]))
    return pairs


def exchange(value, axis, mask):
    return lax.ppermute(value, AXES, flip(axis, mask))


def split(value):
    high = value.astype(jnp.bfloat16)
    return high, (value - high.astype(jnp.float32)).astype(jnp.bfloat16)


def relayout_kernel(a_ref, out_ref):
    for i in range(NY * NX):
        out_ref[i] = a_ref[:, pl.ds(i * 2 * DEPTH, 2 * DEPTH)]


def relayout(a):
    return pl.pallas_call(
        relayout_kernel,
        out_shape=jax.ShapeDtypeStruct((NY * NX, ROWS, 2 * DEPTH), jnp.float32),
        in_specs=[VMEM],
        out_specs=VMEM,
        compiler_params=pltpu.CompilerParams(vmem_limit_bytes=4 << 20),
        cost_estimate=CHEAP,
    )(a)


def after(value, *earlier):
    return lax.optimization_barrier((value, *earlier))[0]


def columns(group):
    return pl.ds(group * 2 * WIDTH, 2 * WIDTH)


def multiply(group, half, other, hi_ref, lo_ref, b):
    blocks = (NEAR_FIRST, FAR_FIRST)[group % 2]
    order = [(outer, inner) for outer in blocks[2 * half : 2 * half + 2] for inner in SECOND]
    order = [qy * 4 + qx if group < 2 else qx * 4 + qy for qx, qy in order]
    depth = pl.ds(other * DEPTH, DEPTH)
    a_hi, a_lo = (
        jnp.concatenate([ref[q * ROWS : (q + 1) * ROWS, depth] for q in order], 0)
        for ref in (hi_ref, lo_ref)
    )
    b_hi, b_lo = split(b)
    dot = functools.partial(jnp.dot, preferred_element_type=jnp.float32)
    return dot(a_hi, b_hi) + dot(a_lo, b_hi) + dot(a_hi, b_lo)


def whole(group, half, hi_ref, lo_ref, own_ref, oth_ref):
    total = multiply(group, half, 0, hi_ref, lo_ref, own_ref[:, columns(group)])
    return total + multiply(group, half, 1, hi_ref, lo_ref, oth_ref[:, columns(group)])


def first_kernel(where, a_ref, own_ref, oth_ref, *refs):
    *outs, hi_ref, lo_ref = refs
    for q in range(NY * NX):
        source = (where[0] ^ (q // 4)) * 4 + (where[1] ^ (q % 4))
        rows = pl.ds(pl.multiple_of(source * ROWS, ROWS), ROWS)
        to = pl.ds(q * ROWS, ROWS)
        for other in range(2):
            depth = pl.ds(pl.multiple_of((where[2] ^ other) * DEPTH, DEPTH), DEPTH)
            high, low = split(a_ref[rows, depth])
            hi_ref[to, pl.ds(other * DEPTH, DEPTH)] = high
            lo_ref[to, pl.ds(other * DEPTH, DEPTH)] = low
    for group, out_ref in enumerate(outs):
        out_ref[...] = whole(group, 0, hi_ref, lo_ref, own_ref, oth_ref)


def product_kernel(groups, half, *refs):
    for group, out_ref in zip(groups, refs[4:]):
        out_ref[...] = whole(group, half, *refs[:4])


def call(kernel, out_shape, in_specs, limit):
    return pl.pallas_call(
        kernel,
        out_shape=out_shape,
        in_specs=in_specs,
        out_specs=jax.tree.map(lambda _: VMEM, out_shape),
        compiler_params=pltpu.CompilerParams(vmem_limit_bytes=limit << 20),
        cost_estimate=CHEAP,
    )


def products(where, a, own, oth):
    out = jax.ShapeDtypeStruct((8 * ROWS, 2 * WIDTH), jnp.float32)
    part = jax.ShapeDtypeStruct((NY * NX * ROWS, 2 * DEPTH), jnp.bfloat16)
    smem = pl.BlockSpec(memory_space=pltpu.SMEM)
    *sends, hi, lo = call(
        first_kernel, (out,) * 2 + (part, part), [smem, VMEM, VMEM, VMEM], 6
    )(where, a, own, oth)
    later = functools.partial(product_kernel, (2, 3), 0)
    sends += call(later, (out,) * 2, [VMEM] * 4, 6)(hi, lo, own, oth)
    hi = after(hi, sends[-1])
    keeps = []
    for group in range(GROUPS):
        kernel = functools.partial(product_kernel, (group,), 1)
        keeps += call(kernel, (out,), [VMEM] * 4, 6)(hi, lo, own, oth)
    return sends, keeps


def body(amplitudes, integrals):
    z, y, x, core = (lax.axis_index(name) for name in AXES)
    where = jnp.stack([y, x, core]).astype(jnp.int32)
    halves = [((z & 1) ^ v) * 4 * WIDTH for v in range(2)]
    blocks = [((z >> 1) ^ v) * WIDTH for v in range(4)]
    scalars = (where, halves, blocks)
    scalars, amplitudes, integrals = lax.optimization_barrier((scalars, amplitudes, integrals))
    where, halves, blocks = scalars
    oth = exchange(integrals, "core", 1)
    laid = relayout(amplitudes)
    mine = lax.all_to_all(laid, ("y", "x"), split_axis=0, concat_axis=0)
    mine = mine.reshape(NY * NX * ROWS, 2 * DEPTH)
    sends, parts = products(where, mine, integrals, oth)
    parts[0] = after(parts[0], *parts[1:])
    last = None
    for step in range(2):
        for group in range(GROUPS):
            keep = parts[group] if last is None else after(parts[group], last)
            mask = ((1, 3), (3, 1))[group % 2][step]
            last = keep + exchange(sends[group], "xxyy"[group], mask)
            if step == 0:
                sends[group], parts[group] = last[: 4 * ROWS], last[4 * ROWS :]
            else:
                parts[group] = last
    pairs = []
    for first, axis in ((0, "y"), (2, "x")):
        pair = [
            jnp.concatenate([part[i * ROWS : (i + 1) * ROWS] for part in parts[first : first + 2]], 1)
            for i in range(4)
        ]
        pairs.append(pair[3] + sum(exchange(pair[i], axis, SECOND[i]) for i in range(3)))
    cut = functools.partial(lax.dynamic_slice_in_dim, axis=1, allow_negative_indices=False)
    order = [(pair, i) for parity in range(2) for pair in pairs for i in (parity, parity + 2)]
    both = jnp.concatenate([pair[:, i * WIDTH : (i + 1) * WIDTH] for pair, i in order], 1)
    keep, send = (cut(both, start, 4 * WIDTH) for start in halves)
    keep = keep + exchange(send, "z", 1)
    block = lambda v: cut(keep, blocks[v], WIDTH)
    far = [exchange(block(v), "z", 2 * v) for v in (2, 1, 3)]
    return 0.5 * (block(0) + far[0] + far[1] + far[2])


def solution(mesh):
    chips = Mesh(mesh.devices.reshape(NZ, NY, NX, 2), AXES)
    return jax.shard_map(
        body,
        mesh=chips,
        in_specs=(P(("y", "x", "core"), "z"), P(AXES, None)),
        out_specs=P(("y", "x", "core"), "z"),
        check_vma=False,
    )
```

```python
import functools

import jax
import jax.numpy as jnp
from jax import lax
from jax.experimental import pallas as pl
from jax.experimental.pallas import tpu as pltpu
from jax.sharding import Mesh, PartitionSpec as P

AXES = ("z", "y", "x", "core")
NZ, NY, NX = 8, 4, 4
ROWS, DEPTH, WIDTH = 32, 512, 384
GROUPS = 4
NEAR_FIRST, FAR_FIRST = (2, 1, 3, 0), (2, 3, 1, 0)
SECOND = (2, 1, 3, 0)
CHEAP = pl.CostEstimate(flops=1 << 20, bytes_accessed=1 << 16, transcendentals=0)
VMEM = pl.BlockSpec(memory_space=pltpu.VMEM)


def flip(axis, mask):
    pairs = []
    for i in range(NZ * NY * NX * 2):
        at = {"z": i // 32, "y": i // 8 % 4, "x": i // 2 % 4, "core": i % 2}
        at[axis] ^= mask
        pairs.append((i, ((at["z"] * 4 + at["y"]) * 4 + at["x"]) * 2 + at["core"]))
    return pairs


def exchange(value, axis, mask):
    return lax.ppermute(value, AXES, flip(axis, mask))


def split(value):
    high = value.astype(jnp.bfloat16)
    return high, (value - high.astype(jnp.float32)).astype(jnp.bfloat16)


def relayout_kernel(a_ref, out_ref):
    for i in range(NY * NX):
        out_ref[i] = a_ref[:, pl.ds(i * 2 * DEPTH, 2 * DEPTH)]


def relayout(a):
    return pl.pallas_call(
        relayout_kernel,
        out_shape=jax.ShapeDtypeStruct((NY * NX, ROWS, 2 * DEPTH), jnp.float32),
        in_specs=[VMEM],
        out_specs=VMEM,
        compiler_params=pltpu.CompilerParams(vmem_limit_bytes=4 << 20),
        cost_estimate=CHEAP,
    )(a)


def after(value, *earlier):
    return lax.optimization_barrier((value, *earlier))[0]


def columns(group):
    return pl.ds(group * 2 * WIDTH, 2 * WIDTH)


def multiply(group, half, other, hi_ref, lo_ref, b):
    blocks = (NEAR_FIRST, FAR_FIRST)[group % 2]
    order = [(outer, inner) for outer in blocks[2 * half : 2 * half + 2] for inner in SECOND]
    order = [qx * 4 + qy if group < 2 else qy * 4 + qx for qx, qy in order]
    depth = pl.ds(other * DEPTH, DEPTH)
    a_hi, a_lo = (
        jnp.concatenate([ref[q * ROWS : (q + 1) * ROWS, depth] for q in order], 0)
        for ref in (hi_ref, lo_ref)
    )
    b_hi, b_lo = split(b)
    dot = functools.partial(jnp.dot, preferred_element_type=jnp.float32)
    return dot(a_hi, b_hi) + dot(a_lo, b_hi) + dot(a_hi, b_lo)


def whole(group, half, hi_ref, lo_ref, own_ref, oth_ref):
    total = multiply(group, half, 0, hi_ref, lo_ref, own_ref[:, columns(group)])
    return total + multiply(group, half, 1, hi_ref, lo_ref, oth_ref[:, columns(group)])


def first_kernel(where, a_ref, own_ref, oth_ref, *refs):
    *outs, hi_ref, lo_ref = refs
    for q in range(NY * NX):
        source = (where[0] ^ (q // 4)) * 4 + (where[1] ^ (q % 4))
        rows = pl.ds(pl.multiple_of(source * ROWS, ROWS), ROWS)
        to = pl.ds(q * ROWS, ROWS)
        for other in range(2):
            depth = pl.ds(pl.multiple_of((where[2] ^ other) * DEPTH, DEPTH), DEPTH)
            high, low = split(a_ref[rows, depth])
            hi_ref[to, pl.ds(other * DEPTH, DEPTH)] = high
            lo_ref[to, pl.ds(other * DEPTH, DEPTH)] = low
    for group, out_ref in enumerate(outs):
        out_ref[...] = whole(group, 0, hi_ref, lo_ref, own_ref, oth_ref)


def product_kernel(groups, half, *refs):
    for group, out_ref in zip(groups, refs[4:]):
        out_ref[...] = whole(group, half, *refs[:4])


def call(kernel, out_shape, in_specs, limit):
    return pl.pallas_call(
        kernel,
        out_shape=out_shape,
        in_specs=in_specs,
        out_specs=jax.tree.map(lambda _: VMEM, out_shape),
        compiler_params=pltpu.CompilerParams(vmem_limit_bytes=limit << 20),
        cost_estimate=CHEAP,
    )


def products(where, a, own, oth):
    out = jax.ShapeDtypeStruct((8 * ROWS, 2 * WIDTH), jnp.float32)
    part = jax.ShapeDtypeStruct((NY * NX * ROWS, 2 * DEPTH), jnp.bfloat16)
    smem = pl.BlockSpec(memory_space=pltpu.SMEM)
    *sends, hi, lo = call(
        first_kernel, (out,) * 2 + (part, part), [smem, VMEM, VMEM, VMEM], 6
    )(where, a, own, oth)
    later = functools.partial(product_kernel, (2, 3), 0)
    sends += call(later, (out,) * 2, [VMEM] * 4, 6)(hi, lo, own, oth)
    hi = after(hi, sends[-1])
    keeps = []
    for group in range(GROUPS):
        kernel = functools.partial(product_kernel, (group,), 1)
        keeps += call(kernel, (out,), [VMEM] * 4, 6)(hi, lo, own, oth)
    return sends, keeps


def body(amplitudes, integrals):
    z, y, x, core = (lax.axis_index(name) for name in AXES)
    where = jnp.stack([y, x, core]).astype(jnp.int32)
    halves = [((z & 1) ^ v) * 4 * WIDTH for v in range(2)]
    blocks = [((z >> 1) ^ v) * WIDTH for v in range(4)]
    scalars = (where, halves, blocks)
    scalars, amplitudes, integrals = lax.optimization_barrier((scalars, amplitudes, integrals))
    where, halves, blocks = scalars
    oth = exchange(integrals, "core", 1)
    laid = relayout(amplitudes)
    mine = lax.all_to_all(laid, ("y", "x"), split_axis=0, concat_axis=0)
    mine = mine.reshape(NY * NX * ROWS, 2 * DEPTH)
    sends, parts = products(where, mine, integrals, oth)
    parts[0] = after(parts[0], *parts[1:])
    last = None
    for step in range(2):
        for group in range(GROUPS):
            keep = parts[group] if last is None else after(parts[group], last)
            mask = ((1, 3), (3, 1))[group % 2][step]
            last = keep + exchange(sends[group], "yyxx"[group], mask)
            if step == 0:
                sends[group], parts[group] = last[: 4 * ROWS], last[4 * ROWS :]
            else:
                parts[group] = last
    pairs = []
    for first, axis in ((0, "x"), (2, "y")):
        pair = [
            jnp.concatenate([part[i * ROWS : (i + 1) * ROWS] for part in parts[first : first + 2]], 1)
            for i in range(4)
        ]
        pairs.append(pair[3] + sum(exchange(pair[i], axis, SECOND[i]) for i in range(3)))
    cut = functools.partial(lax.dynamic_slice_in_dim, axis=1, allow_negative_indices=False)
    order = [(pair, i) for parity in range(2) for pair in pairs for i in (parity, parity + 2)]
    both = jnp.concatenate([pair[:, i * WIDTH : (i + 1) * WIDTH] for pair, i in order], 1)
    keep, send = (cut(both, start, 4 * WIDTH) for start in halves)
    keep = keep + exchange(send, "z", 1)
    block = lambda v: cut(keep, blocks[v], WIDTH)
    far = [exchange(block(v), "z", 2 * v) for v in (2, 1, 3)]
    return 0.5 * (block(0) + far[0] + far[1] + far[2])


def solution(mesh):
    chips = Mesh(mesh.devices.reshape(NZ, NY, NX, 2), AXES)
    return jax.shard_map(
        body,
        mesh=chips,
        in_specs=(P(("y", "x", "core"), "z"), P(AXES, None)),
        out_specs=P(("y", "x", "core"), "z"),
        check_vma=False,
    )
```

```python
import functools

import jax
import jax.numpy as jnp
from jax import lax
from jax.experimental import pallas as pl
from jax.experimental.pallas import tpu as pltpu
from jax.sharding import Mesh, PartitionSpec as P

AXES = ("z", "y", "x", "core")
NZ, NY, NX = 8, 4, 4
ROWS, DEPTH, WIDTH = 32, 512, 384
GROUPS = 4
NEAR_FIRST, FAR_FIRST = (2, 1, 3, 0), (2, 3, 1, 0)
SECOND = (2, 1, 3, 0)
CHEAP = pl.CostEstimate(flops=1 << 20, bytes_accessed=1 << 16, transcendentals=0)
VMEM = pl.BlockSpec(memory_space=pltpu.VMEM)


def flip(axis, mask):
    pairs = []
    for i in range(NZ * NY * NX * 2):
        at = {"z": i // 32, "y": i // 8 % 4, "x": i // 2 % 4, "core": i % 2}
        at[axis] ^= mask
        pairs.append((i, ((at["z"] * 4 + at["y"]) * 4 + at["x"]) * 2 + at["core"]))
    return pairs


def exchange(value, axis, mask):
    return lax.ppermute(value, AXES, flip(axis, mask))


def split(value):
    high = value.astype(jnp.bfloat16)
    return high, (value - high.astype(jnp.float32)).astype(jnp.bfloat16)


def relayout_kernel(a_ref, out_ref):
    for i in range(NY * NX):
        out_ref[i] = a_ref[:, pl.ds(i * 2 * DEPTH, 2 * DEPTH)]


def relayout(a):
    return pl.pallas_call(
        relayout_kernel,
        out_shape=jax.ShapeDtypeStruct((NY * NX, ROWS, 2 * DEPTH), jnp.float32),
        in_specs=[VMEM],
        out_specs=VMEM,
        compiler_params=pltpu.CompilerParams(vmem_limit_bytes=4 << 20),
        cost_estimate=CHEAP,
    )(a)


def after(value, *earlier):
    return lax.optimization_barrier((value, *earlier))[0]


def columns(group):
    return pl.ds(group * 2 * WIDTH, 2 * WIDTH)


def multiply(group, half, other, hi_ref, lo_ref, b):
    blocks = (NEAR_FIRST, FAR_FIRST)[group % 2]
    order = [(outer, inner) for outer in blocks[2 * half : 2 * half + 2] for inner in SECOND]
    order = [qy * 4 + qx if group < 2 else qx * 4 + qy for qx, qy in order]
    depth = pl.ds(other * DEPTH, DEPTH)
    a_hi, a_lo = (
        jnp.concatenate([ref[q * ROWS : (q + 1) * ROWS, depth] for q in order], 0)
        for ref in (hi_ref, lo_ref)
    )
    b_hi, b_lo = split(b)
    dot = functools.partial(jnp.dot, preferred_element_type=jnp.float32)
    return dot(a_hi, b_hi) + dot(a_lo, b_hi) + dot(a_hi, b_lo)


def whole(group, half, hi_ref, lo_ref, own_ref, oth_ref):
    total = multiply(group, half, 0, hi_ref, lo_ref, own_ref[:, columns(group)])
    return total + multiply(group, half, 1, hi_ref, lo_ref, oth_ref[:, columns(group)])


def first_kernel(where, a_ref, own_ref, oth_ref, *refs):
    *outs, hi_ref, lo_ref = refs
    for q in range(NY * NX):
        source = (where[0] ^ (q // 4)) * 4 + (where[1] ^ (q % 4))
        rows = pl.ds(pl.multiple_of(source * ROWS, ROWS), ROWS)
        to = pl.ds(q * ROWS, ROWS)
        for other in range(2):
            depth = pl.ds(pl.multiple_of((where[2] ^ other) * DEPTH, DEPTH), DEPTH)
            high, low = split(a_ref[rows, depth])
            hi_ref[to, pl.ds(other * DEPTH, DEPTH)] = high
            lo_ref[to, pl.ds(other * DEPTH, DEPTH)] = low
    for group, out_ref in enumerate(outs):
        out_ref[...] = whole(group, 0, hi_ref, lo_ref, own_ref, oth_ref)


def product_kernel(groups, half, *refs):
    for group, out_ref in zip(groups, refs[4:]):
        out_ref[...] = whole(group, half, *refs[:4])


def call(kernel, out_shape, in_specs, limit):
    return pl.pallas_call(
        kernel,
        out_shape=out_shape,
        in_specs=in_specs,
        out_specs=jax.tree.map(lambda _: VMEM, out_shape),
        compiler_params=pltpu.CompilerParams(vmem_limit_bytes=limit << 20),
        cost_estimate=CHEAP,
    )


def products(where, a, own, oth):
    out = jax.ShapeDtypeStruct((8 * ROWS, 2 * WIDTH), jnp.float32)
    part = jax.ShapeDtypeStruct((NY * NX * ROWS, 2 * DEPTH), jnp.bfloat16)
    smem = pl.BlockSpec(memory_space=pltpu.SMEM)
    *sends, hi, lo = call(
        first_kernel, (out,) * 2 + (part, part), [smem, VMEM, VMEM, VMEM], 6
    )(where, a, own, oth)
    later = functools.partial(product_kernel, (2, 3), 0)
    sends += call(later, (out,) * 2, [VMEM] * 4, 6)(hi, lo, own, oth)
    hi = after(hi, sends[-1])
    keeps = []
    for group in range(GROUPS):
        kernel = functools.partial(product_kernel, (group,), 1)
        keeps += call(kernel, (out,), [VMEM] * 4, 6)(hi, lo, own, oth)
    return sends, keeps


def body(amplitudes, integrals):
    z, y, x, core = (lax.axis_index(name) for name in AXES)
    where = jnp.stack([y, x, core]).astype(jnp.int32)
    halves = [((z & 1) ^ v) * 4 * WIDTH for v in range(2)]
    blocks = [((z >> 1) ^ v) * WIDTH for v in range(4)]
    scalars = (where, halves, blocks)
    scalars, amplitudes, integrals = lax.optimization_barrier((scalars, amplitudes, integrals))
    where, halves, blocks = scalars
    oth = exchange(integrals, "core", 1)
    laid = relayout(amplitudes)
    mine = lax.all_to_all(laid, ("y", "x"), split_axis=0, concat_axis=0)
    mine = mine.reshape(NY * NX * ROWS, 2 * DEPTH)
    sends, parts = products(where, mine, integrals, oth)
    parts[0] = after(parts[0], *parts[1:])
    last = None
    for step in range(2):
        for group in range(GROUPS):
            keep = parts[group] if last is None else after(parts[group], last)
            mask = ((1, 3), (3, 1))[group % 2][step]
            last = keep + exchange(sends[group], "xxyy"[group], mask)
            if step == 0:
                sends[group], parts[group] = last[: 4 * ROWS], last[4 * ROWS :]
            else:
                parts[group] = last
    pairs = []
    for first, axis in ((0, "y"), (2, "x")):
        pair = [
            jnp.concatenate([part[i * ROWS : (i + 1) * ROWS] for part in parts[first : first + 2]], 1)
            for i in range(4)
        ]
        pairs.append(pair[3] + sum(exchange(pair[i], axis, SECOND[i]) for i in range(3)))
    cut = functools.partial(lax.dynamic_slice_in_dim, axis=1, allow_negative_indices=False)
    order = [(pair, i) for parity in range(2) for pair in pairs for i in (parity, parity + 2)]
    both = jnp.concatenate([pair[:, i * WIDTH : (i + 1) * WIDTH] for pair, i in order], 1)
    keep, send = (cut(both, start, 4 * WIDTH) for start in halves)
    keep = keep + exchange(send, "z", 1)
    block = lambda v: cut(keep, blocks[v], WIDTH)
    far = [exchange(block(v), "z", 2 * v) for v in (2, 3, 1)]
    return 0.5 * (block(0) + far[0] + far[1] + far[2])


def solution(mesh):
    chips = Mesh(mesh.devices.reshape(NZ, NY, NX, 2), AXES)
    return jax.shard_map(
        body,
        mesh=chips,
        in_specs=(P(("y", "x", "core"), "z"), P(AXES, None)),
        out_specs=P(("y", "x", "core"), "z"),
        check_vma=False,
    )
```
